32 devices in a mesh: fsdp: 16 (over z, x, core), seq: 2 (over y).
Axes of the slice: x: 2, y: 2, z: 4, core: 2. Of those that a mesh axis runs over, the one named last changes fastest.
Arguments:
- latents: bfloat16 [16, 1024, 1152], P('fsdp', 'seq'), may hold values from -6 to 6
- condition: bfloat16 [16, 1152], P('fsdp'), may hold values from -6 to 6
- w_ada: bfloat16 [1152, 6912], P('fsdp'), may hold values from -0.1875 to 0.1875
- b_ada: bfloat16 [6912], P('fsdp'), may hold values from -2 to 2
- w_qkv: bfloat16 [1152, 3456], P('fsdp'), may hold values from -0.1875 to 0.1875
- b_qv: bfloat16 [2304], P('fsdp'), may hold values from -2 to 2
- w_proj: bfloat16 [1152, 1152], P('fsdp'), may hold values from -1.5 to 1.5
- b_proj: bfloat16 [1152], P('fsdp'), may hold values from -2 to 2
- w_fc1: bfloat16 [1152, 4608], P('fsdp'), may hold values from -0.1875 to 0.1875
- b_fc1: bfloat16 [4608], P('fsdp'), may hold values from -2 to 2
- w_fc2: bfloat16 [4608, 1152], P('fsdp'), may hold values from -0.09375 to 0.09375
- b_fc2: bfloat16 [1152], P('fsdp'), may hold values from -2 to 2
- grad_out: bfloat16 [16, 1024, 1152], P('fsdp', 'seq'), may hold values from -6 to 6
Outputs:
- output: bfloat16 [16, 1024, 1152], P('fsdp', 'seq')
- grad_latents: float32 [16, 1024, 1152], P('fsdp', 'seq')
- grad_condition: float32 [16, 1152], P('fsdp')
- grad_w_ada: float32 [1152, 6912], P('fsdp')
- grad_b_ada: float32 [6912], P('fsdp')
- grad_w_qkv: float32 [1152, 3456], P('fsdp')
- grad_b_qv: float32 [2304], P('fsdp')
- grad_w_proj: float32 [1152, 1152], P('fsdp')
- grad_b_proj: float32 [1152], P('fsdp')
- grad_w_fc1: float32 [1152, 4608], P('fsdp')
- grad_b_fc1: float32 [4608], P('fsdp')
- grad_w_fc2: float32 [4608, 1152], P('fsdp')
- grad_b_fc2: float32 [1152], P('fsdp')
The draws below stay inside these ranges and needn't reach their ends.
All inputs are finite; a program needn't handle non-finite values.
Results may differ from the reference program's by a relative error of at most 0.018.
Values may be sent and summed in bfloat16 or wider, within the bound.
A program may use at most 256 MiB of HBM per device.

```python
import math
from functools import partial
import jax
import jax.numpy as jnp
from jax import lax

D = 1152
HEADS = 16
HD = 72
FF = 4608
SEQLEN = 1024
LATENTS = 16


def spiked(values, rng, source, target, parts, factor):
    owner, partner = [(jnp.arange(values.shape[dim]) // (values.shape[dim] // parts)).reshape([-1 if axis == dim else 1 for axis in range(values.ndim)]) for dim in (source, target)]
    chosen = jax.random.permutation(rng, parts)[partner]
    strong = (owner == chosen) | (owner == (partner + parts // 2) % parts)
    return jnp.where(strong, factor * values, values)


def levels(stream_key, shape, shards, smallest, top_value):
    level, own = 1.0, jax.random.fold_in(stream_key, 6)
    for position, parts in shards:
        heights = jnp.exp(jax.random.uniform(jax.random.fold_in(own, position), (parts,), jnp.float32, smallest / len(shards), top_value / len(shards)))
        level = level * jnp.repeat(heights, shape[position] // parts).reshape([-1 if axis == position else 1 for axis in range(len(shape))])
    return level


def scatter_about(stream_key, shape, scale, most, shards=(), dtype=jnp.bfloat16):
    level = levels(stream_key, shape, shards, -0.22, 0.18) if shards else 1.0
    values = jax.random.normal(stream_key, shape, jnp.float32) * scale * level
    return jnp.minimum(jnp.maximum(values, -most), most).astype(dtype)


def heavy_noise(rng, shape, scale, reach, shards, heavy, kind=jnp.bfloat16):
    values = scale * jax.random.normal(rng, shape, jnp.float32)
    if shards:
        values = values * levels(rng, shape, shards, -0.22, 0.18)
    return jnp.clip(spiked(values, jax.random.fold_in(rng, 3), *heavy), -reach, reach).astype(kind)


def setup_inputs(seed: int = 0) -> dict:
    key_of = jax.random.split(jax.random.key(seed), 14)
    return {
        "latents": heavy_noise(key_of[0], (LATENTS, SEQLEN, D), 1.0, 6.0, ((0, 16), (1, 2)), (0, 2, 16, 2.0)),
        "condition": scatter_about(key_of[1], (LATENTS, D), 1.0, 6.0, ((0, 16),)),
        "w_ada": scatter_about(key_of[2], (D, 6 * D), D ** -0.5, 0.1875, ((0, 16),)),
        "b_ada": scatter_about(key_of[3], (6 * D,), 0.3, 2.0, ((0, 16),)),
        "w_qkv": scatter_about(key_of[4], (D, 3 * D), D ** -0.5, 0.1875, ((0, 16),)),
        "b_qv": scatter_about(key_of[5], (2 * D,), 0.3, 2.0, ((0, 16),)),
        "w_proj": scatter_about(key_of[6], (D, D), (D * 16 // SEQLEN) ** -0.5, 1.5, ((0, 16),)),
        "b_proj": scatter_about(key_of[7], (D,), 0.3, 2.0, ((0, 16),)),
        "w_fc1": scatter_about(key_of[8], (D, FF), D ** -0.5, 0.1875, ((0, 16),)),
        "b_fc1": scatter_about(key_of[9], (FF,), 0.3, 2.0, ((0, 16),)),
        "w_fc2": scatter_about(key_of[10], (FF, D), FF ** -0.5, 0.09375, ((0, 16),)),
        "b_fc2": scatter_about(key_of[11], (D,), 0.3, 2.0, ((0, 16),)),
        "grad_out": scatter_about(key_of[12], (LATENTS, SEQLEN, D), 1.0, 6.0, ((0, 16), (1, 2))),
    }


@jax.custom_vjp
def low(v):
    return lax.optimization_barrier(v.astype(jnp.bfloat16)).astype(jnp.float32)

@jax.custom_vjp
def low_back(v):
    return v

def low_keep(v):
    return (low(v), None)

def low_pass(kept, grad):
    return (grad,)

def back_keep(v):
    return (v, None)

def back_low(kept, grad):
    return (low(grad),)
low.defvjp(low_keep, low_pass)
low_back.defvjp(back_keep, back_low)
highest = lax.Precision.HIGHEST

def matmul(left, right):
    return jnp.dot(left, right, precision=highest)

def layer_norm(vector):
    centred = vector - lax.optimization_barrier(jnp.mean(vector, axis=-1, keepdims=True))
    spread = lax.optimization_barrier(jnp.mean(centred * centred, axis=-1, keepdims=True))
    return centred * lax.rsqrt(spread + 1e-06)

def sigmoid_linear(vector):
    return vector / (1.0 + jnp.exp(-vector))

def gelu_tanh(vector):
    return 0.5 * vector * (1.0 + jnp.tanh(0.7978845608028654 * (vector + 0.044715 * vector * vector * vector)))

def latent_block(weights, inputs):
    w_qkv, b_qv, w_proj, b_proj, w_fc1, b_fc1, w_fc2, b_fc2 = weights
    tokens, modulation = inputs
    shift_a, scale_a, gate_a, shift_m, scale_m, gate_m = jnp.split(modulation, 6)
    normed = low(layer_norm(tokens) * (1.0 + scale_a) + shift_a)
    bias_all = jnp.concatenate([b_qv[:D], jnp.zeros((D,), jnp.float32), b_qv[D:]])
    joined = (matmul(normed, w_qkv) + bias_all).reshape(SEQLEN, 3, HEADS, HD)
    query = low_back(low(joined[:, 0]))
    key_rows = low_back(low(joined[:, 1]))
    values = low_back(low(joined[:, 2]))
    scores = low_back(jnp.einsum('qhd,khd->hqk', query, key_rows, precision=highest) / math.sqrt(HD))
    row_max = lax.optimization_barrier(jnp.max(scores, axis=-1, keepdims=True))
    exponent = jnp.exp(scores - row_max)
    probabilities = exponent / lax.optimization_barrier(jnp.sum(exponent, axis=-1, keepdims=True))
    mixture = jnp.einsum('hqk,khd->qhd', low(probabilities), values, precision=highest).reshape(SEQLEN, D)
    attended = low_back(low(mixture))
    branch_a = low_back(matmul(attended, w_proj) + b_proj)
    middle = tokens + gate_a * branch_a
    normed_m = low(layer_norm(middle) * (1.0 + scale_m) + shift_m)
    hidden = low_back(matmul(normed_m, w_fc1) + b_fc1)
    active = low(gelu_tanh(hidden))
    branch_m = low_back(matmul(active, w_fc2) + b_fc2)
    return middle + gate_m * branch_m

def forward(latents, condition, w_ada, b_ada, w_qkv, b_qv, w_proj, b_proj, w_fc1, b_fc1, w_fc2, b_fc2):
    modulation = low_back(matmul(low(sigmoid_linear(condition)), w_ada) + b_ada)
    weights = (w_qkv, b_qv, w_proj, b_proj, w_fc1, b_fc1, w_fc2, b_fc2)
    return lax.map(jax.checkpoint(partial(latent_block, weights)), (latents, modulation))

def reference(latents, condition, w_ada, b_ada, w_qkv, b_qv, w_proj, b_proj, w_fc1, b_fc1, w_fc2, b_fc2, grad_out):
    result, pull = jax.vjp(forward, latents.astype(jnp.float32), condition.astype(jnp.float32), w_ada.astype(jnp.float32), b_ada.astype(jnp.float32), w_qkv.astype(jnp.float32), b_qv.astype(jnp.float32), w_proj.astype(jnp.float32), b_proj.astype(jnp.float32), w_fc1.astype(jnp.float32), b_fc1.astype(jnp.float32), w_fc2.astype(jnp.float32), b_fc2.astype(jnp.float32))
    grads = pull(grad_out.astype(jnp.float32))
    return (result.astype(jnp.bfloat16), grads[0], grads[1], grads[2], grads[3], grads[4], grads[5], grads[6], grads[7], grads[8], grads[9], grads[10], grads[11])
```

```python
import math

import jax
import jax.numpy as jnp
from jax import lax
from jax.experimental import pallas as pl
from jax.experimental.pallas import tpu as pltpu
from jax.sharding import PartitionSpec as P

HD = 72
PAIR = 2 * HD
FACTOR = 1.0 / math.sqrt(HD)
FLOAT = jnp.float32
LOW = jnp.bfloat16
SWAP = [(0, 1), (1, 0)]


def contract(left, right, left_dim, right_dim):
    return lax.dot_general(
        left, right, (((left_dim,), (right_dim,)), ((), ())), preferred_element_type=FLOAT
    )


def exponentials(keys, query):
    scores = contract(keys, query, 0, 0)
    row_max = jnp.max(scores, axis=0, keepdims=True)
    exponent = jnp.exp((scores - row_max) * FACTOR)
    return exponent, 1.0 / jnp.sum(exponent, axis=0, keepdims=True)


def attend_kernel(query_ref, key_ref, value_ref, out_ref):
    query, keys, values = query_ref[0], key_ref[0], value_ref[0]
    row = lax.broadcasted_iota(jnp.int32, query.shape, 0)
    total = jnp.zeros(query.shape, FLOAT)
    for head in range(2):
        mine = (row < HD) if head == 0 else (row >= HD)
        masked = jnp.where(mine, query.astype(FLOAT), 0.0).astype(LOW)
        exponent, inverse = exponentials(keys, masked)
        mixture = contract(values, exponent.astype(LOW), 1, 0) * inverse
        total = total + jnp.where(mine, mixture, 0.0)
    out_ref[0] = total.astype(LOW)


def revisit_kernel(query_ref, key_ref, value_ref, grad_ref, dq_ref, dk_ref, dv_ref):
    query, keys, values, grad = query_ref[0], key_ref[0], value_ref[0], grad_ref[0]
    row = lax.broadcasted_iota(jnp.int32, query.shape, 0)
    d_query = jnp.zeros(query.shape, FLOAT)
    d_keys = jnp.zeros(keys.shape, FLOAT)
    d_values = jnp.zeros(keys.shape, FLOAT)
    for head in range(2):
        mine = (row < HD) if head == 0 else (row >= HD)
        masked = jnp.where(mine, query.astype(FLOAT), 0.0).astype(LOW)
        grad_masked = jnp.where(mine, grad.astype(FLOAT), 0.0).astype(LOW)
        exponent, inverse = exponentials(keys, masked)
        probs = exponent * inverse
        d_values = d_values + contract(grad_masked, probs.astype(LOW), 1, 1)
        d_probs = contract(values, grad_masked, 0, 0)
        centre = jnp.sum(probs * d_probs, axis=0, keepdims=True)
        d_scores = (probs * (d_probs - centre)).astype(LOW)
        d_query = d_query + jnp.where(mine, contract(keys, d_scores, 1, 0), 0.0)
        d_keys = d_keys + contract(masked, d_scores, 1, 1)
    dq_ref[0] = (d_query * FACTOR).astype(LOW)
    dk_ref[0] = (d_keys * FACTOR).astype(LOW)
    dv_ref[0] = d_values.astype(LOW)


def pair_spec(tokens, offset=0):
    return pl.BlockSpec((1, PAIR, tokens), lambda b, h: (b, h + offset, 0))


def attend(query, key_values):
    group, width, rows = query.shape
    length, pairs = key_values.shape[2], width // PAIR
    scores = group * width * rows * length
    return pl.pallas_call(
        attend_kernel,
        grid=(group, pairs),
        in_specs=[pair_spec(rows), pair_spec(length), pair_spec(length, pairs)],
        out_specs=pair_spec(rows),
        out_shape=jax.ShapeDtypeStruct(query.shape, LOW),
        compiler_params=pltpu.CompilerParams(vmem_limit_bytes=40 * 2**20),
        cost_estimate=pl.CostEstimate(
            flops=24 * scores, bytes_accessed=8 * query.size, transcendentals=scores // HD
        ),
    )(query, key_values, key_values)


def revisit(query, key_values, grad):
    group, width, rows = query.shape
    length, pairs = key_values.shape[2], width // PAIR
    scores = group * width * rows * length
    long_shape = jax.ShapeDtypeStruct((group, width, length), LOW)
    return pl.pallas_call(
        revisit_kernel,
        grid=(group, pairs),
        in_specs=[
            pair_spec(rows),
            pair_spec(length),
            pair_spec(length, pairs),
            pair_spec(rows),
        ],
        out_specs=(pair_spec(rows), pair_spec(length), pair_spec(length)),
        out_shape=(jax.ShapeDtypeStruct(query.shape, LOW), long_shape, long_shape),
        compiler_params=pltpu.CompilerParams(vmem_limit_bytes=40 * 2**20),
        cost_estimate=pl.CostEstimate(
            flops=48 * scores, bytes_accessed=16 * query.size, transcendentals=scores // HD
        ),
    )(query, key_values, key_values, grad)


def layer_norm(vector):
    centred = vector - jnp.mean(vector, axis=-1, keepdims=True)
    spread = jnp.mean(centred * centred, axis=-1, keepdims=True)
    return centred * lax.rsqrt(spread + 1e-06)


def modulate(vector, shift, scale):
    return layer_norm(vector) * (1.0 + scale[:, None, :]) + shift[:, None, :]


def sigmoid_linear(vector):
    return vector / (1.0 + jnp.exp(-vector))


def gelu_tanh(vector):
    return (
        0.5
        * vector
        * (1.0 + jnp.tanh(0.7978845608028654 * (vector + 0.044715 * vector * vector * vector)))
    )


def per_device(
    latents,
    condition,
    w_ada,
    b_ada,
    w_qkv,
    b_qv,
    w_proj,
    b_proj,
    w_fc1,
    b_fc1,
    w_fc2,
    b_fc2,
    grad_out,
):
    shards, halves = lax.axis_size("fsdp"), lax.axis_size("seq")
    shard, side = lax.axis_index("fsdp"), lax.axis_index("seq")
    paired = halves == 2
    model_width = w_proj.shape[1]
    own_rows = w_qkv.shape[0]
    lat_group = latents.shape[0]

    def exchange(value):
        return lax.ppermute(value, "seq", SWAP)

    def seq_sum(value):
        value = value.astype(LOW)
        if paired:
            return value.astype(FLOAT) + exchange(value).astype(FLOAT)
        return lax.psum(value.astype(FLOAT), "seq")

    def to_all(vector):
        spread = jnp.broadcast_to(vector[None], (shards,) + vector.shape)
        return lax.all_to_all(spread, "fsdp", 0, 0, tiled=True)

    def gather(weight):
        return lax.all_gather(weight, "fsdp", axis=0, tiled=True)

    def side_by_side(mine, other, axis):
        first = side == 0
        return jnp.concatenate(
            [jnp.where(first, mine, other), jnp.where(first, other, mine)], axis=axis
        )

    def scatter(value):
        return lax.psum_scatter(value.astype(LOW), "fsdp", scatter_dimension=0, tiled=True)

    if paired:
        half_rows = w_fc2.shape[0] // 2
        half_fc2 = lax.dynamic_slice_in_dim(w_fc2, side * half_rows, half_rows, 0)
        mine_fc2 = gather(half_fc2).reshape(shards, half_rows, model_width)
        full_fc2 = side_by_side(mine_fc2, exchange(mine_fc2), 1).reshape(-1, model_width)
    else:
        full_fc2 = gather(w_fc2)
    full_qkv = gather(w_qkv)
    full_proj = gather(w_proj)
    full_fc1 = gather(w_fc1)

    small = (condition.reshape(-1), b_ada, b_qv, b_proj, b_fc1, b_fc2)
    sizes = [part.shape[0] for part in small]
    packed = to_all(jnp.concatenate(small))
    edges = [sum(sizes[: i + 1]) for i in range(len(sizes) - 1)]
    parts = jnp.split(packed, edges, axis=1)
    all_conditions = parts[0].reshape(shards * lat_group, model_width).astype(FLOAT)
    bias_ada, bias_qv, bias_proj, bias_fc1, bias_fc2 = [
        part.reshape(-1).astype(FLOAT) for part in parts[1:]
    ]
    cond_own = lax.dynamic_slice_in_dim(
        sigmoid_linear(all_conditions).astype(LOW), shard * own_rows, own_rows, 1
    )
    partial_modulation = jnp.dot(cond_own, w_ada, preferred_element_type=FLOAT)
    partial_modulation = lax.all_to_all(
        partial_modulation.reshape(shards, lat_group, -1), "fsdp", 0, 0, tiled=True
    )
    modulation = jnp.sum(partial_modulation, axis=0) + bias_ada
    shift_a, scale_a, gate_a, shift_m, scale_m, gate_m = jnp.split(modulation, 6, axis=1)

    tokens = latents.astype(FLOAT)
    tok_rows = tokens.shape[1]
    normed = modulate(tokens, shift_a, scale_a).astype(LOW)
    bias_kv = jnp.concatenate([jnp.zeros((model_width,), FLOAT), bias_qv[model_width:]])
    own_kv = (
        jnp.einsum("btd,de->bet", normed, full_qkv[:, model_width:], preferred_element_type=FLOAT)
        + bias_kv[:, None]
    ).astype(LOW)
    if paired:
        key_values = jnp.concatenate([own_kv, exchange(own_kv)], axis=2)
    else:
        key_values = lax.all_gather(own_kv, "seq", axis=2, tiled=True)
    query = (
        jnp.einsum("btd,de->bet", normed, full_qkv[:, :model_width], preferred_element_type=FLOAT)
        + bias_qv[:model_width, None]
    ).astype(LOW)
    attended = attend(query, key_values)
    branch_a = jnp.einsum("bdt,de->bte", attended, full_proj, preferred_element_type=FLOAT) + bias_proj
    middle = tokens + gate_a[:, None, :] * branch_a
    normed_m = modulate(middle, shift_m, scale_m).astype(LOW)
    hidden = jnp.einsum("btd,df->btf", normed_m, full_fc1, preferred_element_type=FLOAT) + bias_fc1
    active = gelu_tanh(hidden).astype(LOW)
    cotangent = grad_out.astype(FLOAT)
    d_branch_m = (gate_m[:, None, :] * cotangent).astype(LOW)
    grad_fc2 = jnp.einsum("btf,btd->fd", active, d_branch_m, preferred_element_type=FLOAT)
    owned_fc2 = scatter(grad_fc2)
    branch_m = jnp.einsum("btf,fd->btd", active, full_fc2, preferred_element_type=FLOAT) + bias_fc2
    output = (middle + gate_m[:, None, :] * branch_m).astype(LOW)
    d_gate_m = jnp.sum(cotangent * branch_m, axis=1)
    grad_bias_fc2 = jnp.sum(d_branch_m, axis=(0, 1), dtype=FLOAT)
    d_active = jnp.einsum("btd,fd->btf", d_branch_m, full_fc2, preferred_element_type=FLOAT)
    gelu_unused, gelu_pull = jax.vjp(gelu_tanh, hidden)
    d_hidden = gelu_pull(d_active)[0].astype(LOW)
    grad_bias_fc1 = jnp.sum(d_hidden, axis=(0, 1), dtype=FLOAT)

    def grad_fc1_of(columns):
        return jnp.einsum("btd,btf->df", normed_m, columns, preferred_element_type=FLOAT)

    if paired:
        half = d_hidden.shape[2] // 2
        sent = exchange(
            grad_fc1_of(lax.dynamic_slice_in_dim(d_hidden, (1 - side) * half, half, 2)).astype(LOW)
        )
        kept = grad_fc1_of(lax.dynamic_slice_in_dim(d_hidden, side * half, half, 2))
    else:
        owned_fc1 = seq_sum(scatter(grad_fc1_of(d_hidden)))
    d_normed_m = jnp.einsum("btf,df->btd", d_hidden, full_fc1, preferred_element_type=FLOAT)
    norm_unused, pull_second = jax.vjp(modulate, middle, shift_m, scale_m)
    d_middle_norm, d_shift_m, d_scale_m = pull_second(d_normed_m)
    d_middle = cotangent + d_middle_norm
    d_gate_a = jnp.sum(d_middle * branch_a, axis=1)
    d_branch_a = (gate_a[:, None, :] * d_middle).astype(LOW)
    grad_proj = jnp.einsum("bdt,bte->de", attended, d_branch_a, preferred_element_type=FLOAT)
    owned_proj = scatter(grad_proj)
    grad_bias_proj = jnp.sum(d_branch_a, axis=(0, 1), dtype=FLOAT)
    d_attended = jnp.einsum(
        "bte,de->bdt", d_branch_a, full_proj, preferred_element_type=FLOAT
    ).astype(LOW)
    d_query, d_keys, d_values = revisit(query, key_values, d_attended)
    if paired:
        sent, d_query, d_keys, d_values = lax.optimization_barrier(
            (sent, d_query, d_keys, d_values)
        )
        half_fc1 = scatter(kept + sent.astype(FLOAT))
        owned_fc1 = side_by_side(half_fc1, exchange(half_fc1), 1).astype(FLOAT)
        away = jnp.concatenate([d_keys[:, :, tok_rows:], d_values[:, :, tok_rows:]], axis=1)
        home = jnp.concatenate([d_keys[:, :, :tok_rows], d_values[:, :, :tok_rows]], axis=1)
        d_kv = (home.astype(FLOAT) + exchange(away).astype(FLOAT)).astype(LOW)
    else:
        d_kv = lax.psum_scatter(
            jnp.concatenate([d_keys, d_values], axis=1), "seq", scatter_dimension=2, tiled=True
        )
    d_joined = jnp.concatenate([d_query, d_kv], axis=1)
    grad_qkv = jnp.einsum("btd,bet->de", normed, d_joined, preferred_element_type=FLOAT)
    owned_qkv = scatter(grad_qkv)
    column_sums = jnp.sum(d_joined, axis=(0, 2), dtype=FLOAT)
    grad_bias_qv = jnp.concatenate([column_sums[:model_width], column_sums[2 * model_width :]])
    d_normed_a = jnp.einsum("bet,de->btd", d_joined, full_qkv, preferred_element_type=FLOAT)
    first_unused, pull_first = jax.vjp(modulate, tokens, shift_a, scale_a)
    d_tokens_norm, d_shift_a, d_scale_a = pull_first(d_normed_a)
    grad_latents = d_middle + d_tokens_norm

    d_mod_part = jnp.concatenate(
        [d_shift_a, d_scale_a, d_gate_a, d_shift_m, d_scale_m, d_gate_m], axis=1
    )
    bias_parts = (grad_bias_qv, grad_bias_proj, grad_bias_fc1, grad_bias_fc2)
    chunks = jnp.concatenate([part.reshape(shards, -1) for part in bias_parts], axis=1)
    mod_size = d_mod_part.size
    flat = seq_sum(jnp.concatenate([d_mod_part.reshape(-1), chunks.reshape(-1)])).astype(LOW)
    spread = jnp.concatenate(
        [
            jnp.broadcast_to(flat[None, :mod_size], (shards, mod_size)),
            flat[mod_size:].reshape(shards, -1),
        ],
        axis=1,
    )
    arrived = lax.all_to_all(spread, "fsdp", 0, 0, tiled=True)
    d_modulation = arrived[:, :mod_size].reshape(shards * lat_group, -1)
    owned_chunks = jnp.sum(arrived[:, mod_size:], axis=0, dtype=FLOAT)
    bias_edges = [
        b_qv.shape[0],
        b_qv.shape[0] + b_proj.shape[0],
        b_qv.shape[0] + b_proj.shape[0] + b_fc1.shape[0],
    ]
    owned_qv, owned_bproj, owned_bfc1, owned_bfc2 = jnp.split(owned_chunks, bias_edges)
    owned_ada = jnp.einsum("lk,le->ke", cond_own, d_modulation, preferred_element_type=FLOAT)
    owned_bada = lax.dynamic_slice_in_dim(
        jnp.sum(d_modulation, axis=0, dtype=FLOAT), shard * b_ada.shape[0], b_ada.shape[0], 0
    )
    d_cond = jnp.einsum("le,ke->lk", d_modulation, w_ada, preferred_element_type=FLOAT)
    d_cond = lax.all_to_all(
        d_cond.reshape(shards, lat_group, own_rows), "fsdp", 0, 0, tiled=True
    )
    d_cond = jnp.moveaxis(d_cond, 0, 1).reshape(lat_group, model_width)
    silu_unused, silu_pull = jax.vjp(sigmoid_linear, condition.astype(FLOAT))
    grad_condition = silu_pull(d_cond)[0]
    return (
        output,
        grad_latents,
        grad_condition,
        owned_ada,
        owned_bada,
        seq_sum(owned_qkv),
        owned_qv,
        seq_sum(owned_proj),
        owned_bproj,
        owned_fc1,
        owned_bfc1,
        seq_sum(owned_fc2),
        owned_bfc2,
    )


def solution(mesh):
    return jax.shard_map(
        per_device,
        mesh=mesh,
        in_specs=(
            P("fsdp", "seq", None),
            P("fsdp", None),
            P("fsdp", None),
            P("fsdp"),
            P("fsdp", None),
            P("fsdp"),
            P("fsdp", None),
            P("fsdp"),
            P("fsdp", None),
            P("fsdp"),
            P("fsdp", None),
            P("fsdp"),
            P("fsdp", "seq", None),
        ),
        out_specs=(
            P("fsdp", "seq", None),
            P("fsdp", "seq", None),
            P("fsdp", None),
            P("fsdp", None),
            P("fsdp"),
            P("fsdp", None),
            P("fsdp"),
            P("fsdp", None),
            P("fsdp"),
            P("fsdp", None),
            P("fsdp"),
            P("fsdp", None),
            P("fsdp"),
        ),
        check_vma=False,
    )
```
